32 devices in a mesh: dp: 2 (over core), seq: 16 (over z, y, x).
Axes of the slice: x: 2, y: 2, z: 4, core: 2. Of those that a mesh axis runs over, the one named last changes fastest.
Arguments:
- y_first: bfloat16 [2, 32, 64, 1152], P('dp', 'seq'), may hold values from -10 to 10
- y_second: bfloat16 [2, 32, 64, 1152], P('dp', 'seq'), may hold values from -10 to 10
- grad_first: bfloat16 [2, 32, 64, 1152], P('dp', 'seq'), may hold values from -6 to 6
- grad_second: bfloat16 [2, 32, 64, 1152], P('dp', 'seq'), may hold values from -6 to 6
- w_qkv_space: bfloat16 [1152, 1728], P('seq', 'dp'), may hold values from -1 to 1
- w_out_space: bfloat16 [576, 1152], P('seq', 'dp'), may hold values from -0.25 to 0.25
- w_qkv_time: bfloat16 [1152, 1728], P('seq', 'dp'), may hold values from -1 to 1
- w_out_time: bfloat16 [576, 1152], P('seq', 'dp'), may hold values from -0.25 to 0.25
Outputs:
- x_first: bfloat16 [2, 32, 64, 1152], P('dp', 'seq')
- x_second: bfloat16 [2, 32, 64, 1152], P('dp', 'seq')
- d_first: bfloat16 [2, 32, 64, 1152], P('dp', 'seq')
- d_second: bfloat16 [2, 32, 64, 1152], P('dp', 'seq')
- grad_w_out_time: float32 [576, 1152], P('seq', 'dp')
The draws below stay inside these ranges and needn't reach their ends.
All inputs are finite; a program needn't handle non-finite values.
Results may differ from the reference program's by a relative error of at most 0.025.
Values may be sent and summed in bfloat16 or wider, within the bound.
A program may use at most 64 MiB of HBM per device.

```python
import math
import jax
import jax.numpy as jnp
from jax import lax

D = 1152
HEADS = 8
HD = 72
P_SIZE = 64
FRAMES = 32
CLIPS = 2


def base_tokens(key, salt):
    own = jax.random.fold_in(key, salt)
    return jnp.clip(jax.random.normal(jax.random.fold_in(own, 1), (CLIPS, FRAMES, P_SIZE, D), jnp.float32), -6.0, 6.0)


def base_weights(key, salt):
    own = jax.random.fold_in(key, salt)
    return jnp.clip(jax.random.normal(own, (D, 3 * HEADS * HD), jnp.float32), -4.0, 4.0) * D ** (-0.5)


def draw_y_first(key, part):
    tokens = base_tokens(key, 101)
    return tokens.astype(jnp.bfloat16)


def draw_y_second(key, part):
    tokens = base_tokens(key, 202)
    return tokens.astype(jnp.bfloat16)


def draw_w_qkv_space(key, part):
    weights = base_weights(key, 303)
    return weights.astype(jnp.bfloat16)


def draw_w_qkv_time(key, part):
    weights = base_weights(key, 404)
    return weights.astype(jnp.bfloat16)


def level_of(own_key, extent, split, least, top_value):
    def one(position, blocks):
        heights = jax.random.uniform(jax.random.fold_in(jax.random.fold_in(own_key, 6), position), (blocks,), jnp.float32, least / len(split), top_value / len(split))
        return jnp.repeat(jnp.exp(heights), extent[position] // blocks).reshape((-1,) + (1,) * (len(extent) - position - 1))

    level = one(*split[0])
    for cut in split[1:]:
        level = level * one(*cut)
    return level


def scatter_about(key, dims, deviation, bound, pieces=(), kind=jnp.bfloat16):
    entries = jax.random.normal(key, dims, jnp.float32) * deviation
    if len(pieces) > 0:
        entries = level_of(key, dims, pieces, -0.22, 0.18) * entries
    return jnp.clip(entries, min=-bound, max=bound).astype(kind)


def setup_inputs(seed: int = 0) -> dict:
    key_of = jax.random.split(jax.random.key(seed), 9)
    y_first = draw_y_first(jax.random.fold_in(key_of[8], 71), 0)
    y_second = draw_y_second(jax.random.fold_in(key_of[8], 71), 0)
    grad_first = scatter_about(key_of[2], (CLIPS, FRAMES, P_SIZE, D), 1.0, 6.0, ((0, 2), (1, 16)))
    grad_second = scatter_about(key_of[3], (CLIPS, FRAMES, P_SIZE, D), 1.0, 6.0, ((0, 2), (1, 16)))
    w_qkv_space = draw_w_qkv_space(jax.random.fold_in(key_of[8], 71), 0)
    w_out_space = scatter_about(key_of[5], (HEADS * HD, D), (HEADS * HD) ** -0.5, 0.25, ((0, 16), (1, 2)))
    w_qkv_time = draw_w_qkv_time(jax.random.fold_in(key_of[8], 71), 0)
    w_out_time = scatter_about(key_of[7], (HEADS * HD, D), (HEADS * HD) ** -0.5, 0.25, ((0, 16), (1, 2)))
    return {"y_first": y_first, "y_second": y_second, "grad_first": grad_first, "grad_second": grad_second, "w_qkv_space": w_qkv_space, "w_out_space": w_out_space, "w_qkv_time": w_qkv_time, "w_out_time": w_out_time}


def normalize(values):
    wide = values.astype(jnp.float32)
    scale = lax.rsqrt(lax.optimization_barrier(jnp.mean(wide * wide, axis=-1, keepdims=True)) + 1e-06)
    return (wide * scale).astype(jnp.bfloat16)

def attend(inputs, w_qkv, w_out):
    outer, rows, inner, width = inputs.shape
    normed = normalize(inputs).reshape(-1, width)
    packed = jnp.dot(normed, w_qkv, preferred_element_type=jnp.float32).astype(jnp.bfloat16)
    packed = packed.reshape(outer, rows, inner, 3, HEADS, HD)
    query = packed[:, :, :, 0]
    keys = packed[:, :, :, 1]
    values = packed[:, :, :, 2]
    scores = jnp.einsum('arbhk,asbhk->abhrs', query, keys, preferred_element_type=jnp.float32) / math.sqrt(HD)
    peak = lax.optimization_barrier(jnp.max(scores, axis=-1, keepdims=True))
    expo = jnp.exp(scores - peak)
    probs = (expo / lax.optimization_barrier(jnp.sum(expo, axis=-1, keepdims=True))).astype(jnp.bfloat16)
    mixed = jnp.einsum('abhrs,asbhk->arbhk', probs, values, preferred_element_type=jnp.float32).astype(jnp.bfloat16)
    mixed = mixed.reshape(outer, rows, inner, HEADS * HD)
    result = jnp.dot(mixed.reshape(-1, HEADS * HD), w_out, preferred_element_type=jnp.float32).astype(jnp.bfloat16)
    return (result.reshape(inputs.shape), mixed)

def reference(y_first, y_second, grad_first, grad_second, w_qkv_space, w_out_space, w_qkv_time, w_out_time):

    def one_clip(items):
        first, second, cot_first, cot_second = items

        def time_fn(inputs):
            return attend(inputs, w_qkv_time, w_out_time)

        def space_fn(inputs):
            return attend(inputs, w_qkv_space, w_out_space)[0]
        time_out, time_vjp, time_mixed = jax.vjp(time_fn, first[None], has_aux=True)
        second_in = (second.astype(jnp.float32) - time_out[0].astype(jnp.float32)).astype(jnp.bfloat16)
        space_out, space_vjp = jax.vjp(space_fn, second_in[:, :, None, :])
        first_in = (first.astype(jnp.float32) - space_out[:, :, 0].astype(jnp.float32)).astype(jnp.bfloat16)
        back_time = time_vjp(cot_second[None])[0]
        first_grad = (cot_first.astype(jnp.float32) + back_time[0].astype(jnp.float32)).astype(jnp.bfloat16)
        back_space = space_vjp(first_grad[:, :, None, :])[0]
        second_grad = (cot_second.astype(jnp.float32) + back_space[:, :, 0].astype(jnp.float32)).astype(jnp.bfloat16)
        partial_grad = lax.dot_general(time_mixed.reshape(-1, HEADS * HD), cot_second.reshape(-1, D), (((0,), (0,)), ((), ())), preferred_element_type=jnp.float32)
        return (first_in, second_in, first_grad, second_grad, partial_grad)
    first_in, second_in, first_grad, second_grad, partials = lax.map(one_clip, (y_first, y_second, grad_first, grad_second))
    return (first_in, second_in, first_grad, second_grad, lax.optimization_barrier(jnp.sum(partials, axis=0)))
```

```python
import functools
import math

import jax
import jax.numpy as jnp
from jax import lax
from jax.experimental import pallas as pl
from jax.experimental.pallas import tpu as pltpu
from jax.sharding import PartitionSpec as P

HEADS = 8
HD = 72
WIDE = HEADS * HD
F32 = jnp.float32
BF16 = jnp.bfloat16


def mm(a, b):
    return lax.dot_general(a, b, (((1,), (0,)), ((), ())), preferred_element_type=F32)


def mm_nt(a, b):
    return lax.dot_general(a, b, (((1,), (1,)), ((), ())), preferred_element_type=F32)


def mm_tn(a, b):
    return lax.dot_general(a, b, (((0,), (0,)), ((), ())), preferred_element_type=F32)


def one_hot(rows, columns, target):
    row = lax.broadcasted_iota(jnp.int32, (rows, columns), 0)
    column = lax.broadcasted_iota(jnp.int32, (rows, columns), 1)
    return (target(row) == column).astype(F32).astype(BF16)


def by_head(values, tokens):
    column = lax.broadcasted_iota(jnp.int32, (tokens, WIDE), 1)
    zero = jnp.zeros_like(values)
    return jnp.concatenate(
        [
            jnp.where((column >= h * HD) & (column < (h + 1) * HD), values, zero)
            for h in range(HEADS)
        ],
        axis=0,
    )


def side_by_side(stacked, tokens):
    return jnp.concatenate(
        [stacked[h * tokens : (h + 1) * tokens] for h in range(HEADS)], axis=1
    )


def forward(x, w_q, w_k, w_v, w_out, same):
    tokens = x.shape[0]
    scale = lax.rsqrt(jnp.mean(x * x, axis=-1, keepdims=True) + 1e-06)
    normed = (x * scale).astype(BF16)
    query = by_head(mm(normed, w_q).astype(F32), tokens).astype(BF16)
    keys = mm(normed, w_k).astype(BF16)
    values = mm(normed, w_v).astype(BF16)
    scores = mm_nt(query, keys) * (1.0 / math.sqrt(HD))
    scores = scores.reshape(HEADS, tokens, tokens)
    scores = jnp.where(same[None], scores, -1e30)
    expo = jnp.exp(scores - jnp.max(scores, axis=-1, keepdims=True))
    exact = expo / jnp.sum(expo, axis=-1, keepdims=True)
    probs = exact.reshape(HEADS * tokens, tokens).astype(BF16)
    value_stack = by_head(values.astype(F32), tokens).astype(BF16)
    mixed = mm(side_by_side(probs, tokens), value_stack).astype(BF16)
    result = mm(mixed, w_out).astype(BF16)
    return result, mixed, (x, scale, query, keys, values, probs)


def backward(saved, cotangent, w_q, w_k, w_v, w_out):
    x, scale, query, keys, values, probs = saved
    tokens = x.shape[0]
    d_mixed = mm_nt(cotangent, w_out)
    d_mixed = by_head(d_mixed, tokens).astype(BF16)
    d_values = mm_tn(probs, d_mixed).astype(BF16)
    d_probs = mm_nt(d_mixed, values)
    weight = probs.astype(F32)
    inner = jnp.sum(d_probs * weight, axis=-1, keepdims=True)
    d_scores = (weight * (d_probs - inner) * (1.0 / math.sqrt(HD))).astype(BF16)
    key_stack = by_head(keys.astype(F32), tokens).astype(BF16)
    d_query = mm(side_by_side(d_scores, tokens), key_stack).astype(BF16)
    d_keys = mm_tn(d_scores, query).astype(BF16)
    d_normed = mm_nt(d_query, w_q) + mm_nt(d_keys, w_k) + mm_nt(d_values, w_v)
    inner = jnp.mean(d_normed * x, axis=-1, keepdims=True)
    return d_normed * scale - x * (scale * scale * scale * inner)


def piece_row(t, o, frames, spots, n):
    per = spots // n
    frame, spot = t // spots, t % spots
    return ((spot // per) * 2 + o) * (frames * per) + frame * per + spot % per


def pack_kernel(n, frames, spots, first_ref, second_ref, out_ref):
    tokens = frames * spots
    total = None
    for o, ref in enumerate((first_ref, second_ref)):
        pick = one_hot(
            tokens, 2 * tokens, lambda t: piece_row(t, o, frames, spots, n)
        )
        part = mm_tn(pick, ref[...])
        total = part if total is None else total + part
    out_ref[...] = total.astype(BF16)


def time_kernel(
    half, per, in_ref, q_ref, k_ref, v_ref, w_ref, out_ref, grad_ref
):
    tokens = in_ref.shape[0] // 2
    picks = [
        one_hot(tokens, 2 * tokens, lambda r: ((r // half) * 2 + o) * half + r % half)
        for o in range(2)
    ]
    arrived = in_ref[...]
    x = mm(picks[0], arrived)
    cotangent = mm(picks[1], arrived).astype(BF16)
    row = lax.broadcasted_iota(jnp.int32, (tokens, tokens), 0)
    column = lax.broadcasted_iota(jnp.int32, (tokens, tokens), 1)
    same = row % per == column % per
    w_q, w_k, w_v, w_out = q_ref[...], k_ref[...], v_ref[...], w_ref[...]
    result, mixed, saved = forward(x, w_q, w_k, w_v, w_out, same)
    grad_ref[...] = mm_tn(mixed, cotangent).astype(BF16)
    back = backward(saved, cotangent, w_q, w_k, w_v, w_out).astype(BF16)
    out_ref[...] = (mm_tn(picks[0], result) + mm_tn(picks[1], back)).astype(BF16)


def space_kernel(
    n, frames, spots, in_ref, y1_ref, y2_ref, g1_ref, g2_ref, q_ref, k_ref, v_ref, w_ref,
    x1_ref, x2_ref, d1_ref, d2_ref,
):
    tokens = frames * spots
    arrived = in_ref[...]
    parts = [
        mm(one_hot(tokens, 2 * tokens, lambda t: piece_row(t, o, frames, spots, n)), arrived)
        for o in range(2)
    ]
    row = lax.broadcasted_iota(jnp.int32, (tokens, tokens), 0)
    column = lax.broadcasted_iota(jnp.int32, (tokens, tokens), 1)
    same = row // spots == column // spots
    w_q, w_k, w_v, w_out = q_ref[...], k_ref[...], v_ref[...], w_ref[...]
    x_second = (y2_ref[...].astype(F32) - parts[0]).astype(BF16)
    x2_ref[...] = x_second
    d_first = (g1_ref[...].astype(F32) + parts[1]).astype(BF16)
    d1_ref[...] = d_first
    result, _, saved = forward(x_second.astype(F32), w_q, w_k, w_v, w_out, same)
    x1_ref[...] = (y1_ref[...].astype(F32) - result.astype(F32)).astype(BF16)
    back = backward(saved, d_first, w_q, w_k, w_v, w_out).astype(BF16).astype(F32)
    d2_ref[...] = (g2_ref[...].astype(F32) + back).astype(BF16)


def call(kernel, shapes, *operands):
    many = isinstance(shapes, (tuple, list))
    spec = pl.BlockSpec(memory_space=pltpu.VMEM)
    return pl.pallas_call(
        kernel,
        out_shape=shapes,
        in_specs=[spec] * len(operands),
        out_specs=[spec] * len(shapes) if many else spec,
        compiler_params=pltpu.CompilerParams(vmem_limit_bytes=48 * 2**20),
    )(*operands)


def pack_weights(w_qkv, w_out):
    third = w_out.shape[0] // 3
    cut = w_out.shape[1] // 2
    low, mid, high = w_out[:third], w_out[third : 2 * third], w_out[2 * third :]
    return jnp.concatenate(
        [
            w_qkv,
            jnp.concatenate([low, mid[:, :cut]], axis=1),
            jnp.concatenate([high, mid[:, cut:]], axis=1),
        ],
        axis=0,
    )


def unpack_weights(gathered, rows):
    ndp, n, packed, columns = gathered.shape
    third = (packed - rows) // 2
    wide = columns * 2 // 3
    w_qkv = gathered[:, :, :rows].transpose(1, 2, 0, 3).reshape(n * rows, ndp * columns)
    first = gathered[:, :, rows : rows + third]
    second = gathered[:, :, rows + third :]
    mid = jnp.concatenate([first[..., wide:], second[..., wide:]], axis=-1)
    w_out = jnp.concatenate([first[..., :wide], mid, second[..., :wide]], axis=2)
    w_out = w_out.transpose(1, 2, 0, 3).reshape(n * third * 3, ndp * wide)
    return (w_qkv[:, :WIDE], w_qkv[:, WIDE : 2 * WIDE], w_qkv[:, 2 * WIDE :], w_out)


def gather_weights(w_qkv, w_out, n, ndp):
    packed = pack_weights(w_qkv, w_out)
    rows = lax.all_gather(packed, "seq", axis=0, tiled=True)
    both = lax.all_gather(rows, "dp", axis=0, tiled=True)
    both = both.reshape(ndp, n, packed.shape[0], packed.shape[1])
    return unpack_weights(both, w_qkv.shape[0])


def body(
    n, ndp,
    y_first, y_second, grad_first, grad_second, w_qkv_space, w_out_space, w_qkv_time, w_out_time
):
    shape = y_first.shape
    frames, spots, width = shape[1:]
    tokens = frames * spots
    flat = lambda part: part.reshape(tokens, width)
    like = jax.ShapeDtypeStruct((tokens, width), BF16)
    pair = jax.ShapeDtypeStruct((2 * tokens, width), BF16)
    time_w = gather_weights(w_qkv_time, w_out_time, n, ndp)
    space_w = gather_weights(w_qkv_space, w_out_space, n, ndp)
    per = spots // n
    half = frames * per

    def exchange(rows):
        pieces = rows.reshape(n, 2 * half, width)
        return lax.all_to_all(pieces, "seq", split_axis=0, concat_axis=0, tiled=True).reshape(
            2 * tokens, width
        )

    sent = call(
        functools.partial(pack_kernel, n, frames, spots), pair, flat(y_first), flat(grad_second)
    )
    answer, partial_grad = call(
        functools.partial(time_kernel, half, per),
        (pair, jax.ShapeDtypeStruct((WIDE, width), BF16)),
        exchange(sent), *time_w,
    )
    outs = call(
        functools.partial(space_kernel, n, frames, spots),
        (like,) * 4,
        exchange(answer), flat(y_first), flat(y_second), flat(grad_first), flat(grad_second),
        *space_w,
    )
    columns = width // ndp
    chip = lax.psum_scatter(
        partial_grad.reshape(WIDE, ndp, columns).transpose(1, 0, 2).reshape(ndp * WIDE, columns),
        "dp", scatter_dimension=0, tiled=True,
    )
    pieces = lax.all_to_all(
        chip.reshape(n, WIDE // n, columns), "seq", split_axis=0, concat_axis=0, tiled=True
    )
    grad_share = jnp.sum(pieces.astype(F32), axis=0)
    x1, x2, d1, d2 = [part.reshape(shape) for part in outs]
    return (x1, x2, d1, d2, grad_share)


def solution(mesh):
    tokens = P("dp", "seq", None, None)
    weights = P("seq", "dp")
    return jax.shard_map(
        functools.partial(body, mesh.shape["seq"], mesh.shape["dp"]),
        mesh=mesh,
        in_specs=(tokens,) * 4 + (weights,) * 4,
        out_specs=(tokens,) * 4 + (weights,),
        check_vma=False,
    )
```

```python
import functools
import math

import jax
import jax.numpy as jnp
from jax import lax
from jax.experimental import pallas as pl
from jax.experimental.pallas import tpu as pltpu
from jax.sharding import PartitionSpec as P

HEADS = 8
HD = 72
WIDE = HEADS * HD
F32 = jnp.float32
BF16 = jnp.bfloat16
MESH = pl.DeviceIdType.MESH


def mm(a, b):
    return lax.dot_general(a, b, (((1,), (0,)), ((), ())), preferred_element_type=F32)


def mm_nt(a, b):
    return lax.dot_general(a, b, (((1,), (1,)), ((), ())), preferred_element_type=F32)


def mm_tn(a, b):
    return lax.dot_general(a, b, (((0,), (0,)), ((), ())), preferred_element_type=F32)


def whole(count):
    return (count + 15) // 16 * 16


def one_hot(rows, columns, target):
    place = target(lax.broadcasted_iota(jnp.int32, (rows, 1), 0))
    column = lax.broadcasted_iota(jnp.int32, (rows, columns), 1)
    return jnp.where(column == place, 1.0, 0.0).astype(BF16)


def columns_of(parts, count):
    joined = jnp.concatenate(parts, axis=1) if len(parts) > 1 else parts[0]
    each = joined.shape[1] // count
    return [joined[:, i * each : (i + 1) * each] for i in range(count)]


def forward(x, w_in, w_out, spread_in, spread_out, same):
    tokens = x.shape[0]
    scale = lax.rsqrt(jnp.mean(x * x, axis=-1, keepdims=True) + 1e-06)
    normed = mm((x * scale).astype(BF16), spread_in).astype(BF16)
    query, keys, values = columns_of([mm(normed, w()) for w in w_in], 3)
    query = by_head(query, tokens).astype(BF16)
    scores = mm_nt(query, keys.astype(BF16)) * (1.0 / math.sqrt(HD))
    scores = scores.reshape(HEADS, tokens, tokens)
    scores = jnp.where(same[None], scores, -1e30)
    expo = jnp.exp(scores - jnp.max(scores, axis=-1, keepdims=True))
    exact = expo / jnp.sum(expo, axis=-1, keepdims=True)
    probs = exact.reshape(HEADS * tokens, tokens).astype(BF16)
    mixed = mm(side_by_side(probs, tokens), by_head(values, tokens).astype(BF16)).astype(BF16)
    mixed = mm(mixed, spread_out).astype(BF16)
    result = columns_of([mm(mixed, w()) for w in w_out], 1)[0].astype(BF16)
    return result, mixed, (x, scale, query, keys, values.astype(BF16), probs)


def backward(saved, cotangent, w_in, w_out, spread_in, spread_out):
    x, scale, query, keys, values, probs = saved
    tokens = x.shape[0]
    pieces = columns_of([cotangent], len(w_out))
    d_mixed = sum(mm_nt(piece.astype(BF16), w()) for piece, w in zip(pieces, w_out))
    d_mixed = by_head(mm_nt(d_mixed.astype(BF16), spread_out), tokens).astype(BF16)
    d_values = mm_tn(probs, d_mixed)
    d_probs = mm_nt(d_mixed, values)
    weight = probs.astype(F32)
    inner = jnp.sum(d_probs * weight, axis=-1, keepdims=True)
    d_scores = (weight * (d_probs - inner) * (1.0 / math.sqrt(HD))).astype(BF16)
    d_query = mm(side_by_side(d_scores, tokens), by_head(keys, tokens).astype(BF16))
    d_keys = mm_tn(d_scores, query)
    pieces = columns_of([d_query, d_keys, d_values], len(w_in))
    d_normed = sum(mm_nt(piece.astype(BF16), w()) for piece, w in zip(pieces, w_in))
    d_normed = mm_nt(d_normed.astype(BF16), spread_in)
    inner = jnp.mean(d_normed * x, axis=-1, keepdims=True)
    return d_normed * scale - x * (scale * scale * scale * inner)


def block_kernel(
    n, ndp, frames, spots, rows_in, rows_out,
    y1_ref, y2_ref, g1_ref, g2_ref, ws_ref, os_ref, wt_ref, ot_ref,
    x1_ref, x2_ref, d1_ref, d2_ref, gw_ref,
    w_buf, o_buf, sent, arrived, answer, returned, g_part, g_chip, g_sent, g_arrived,
    w_recv, w_share, p_recv, g_share, send_sems,
):
    quad = 4 if n % 4 == 0 else 1
    line = n // quad
    me_d, me = lax.axis_index("dp"), lax.axis_index("seq")
    z, q = me // quad, me % quad
    x_side, y_side = q + 1 - 2 * (q % 2), (q + 2) % quad
    far = (x_side + 2) % quad
    tokens, width = y1_ref.shape
    per = spots // n
    half = frames * per
    slot = sent.shape[1]
    others = [lax.rem(me + k, n) for k in range(1, n)]
    mates = [lax.rem(me_d + k, ndp) for k in range(1, ndp)]
    first_in, first_out = whole(rows_in), whole(rows_out)
    spans = [
        [(0, first_in), (0, first_out)],
        [(first_in, w_buf.shape[3]), (first_out, o_buf.shape[3])],
    ]
    pending = []

    barrier = pltpu.get_barrier_semaphore()
    for s in others:
        pl.semaphore_signal(barrier, inc=1, device_id=(me_d, s), device_id_type=MESH)
    for d in mates:
        pl.semaphore_signal(barrier, inc=1, device_id=(d, me), device_id_type=MESH)

    def copy(source, target, sem, device):
        made = pltpu.make_async_remote_copy(
            src_ref=source, dst_ref=target, send_sem=send_sems.at[len(pending)],
            recv_sem=sem, device_id=device, device_id_type=MESH,
        )
        made.start()
        pending.append(made)

    def await_into(target, sem):
        pltpu.make_async_remote_copy(
            src_ref=target, dst_ref=target, send_sem=send_sems.at[0], recv_sem=sem,
            device_id=(me_d, others[0]), device_id_type=MESH,
        ).wait_recv()

    def part(phase, kind, zz, qq):
        low, high = spans[phase][kind]
        return (w_buf, o_buf)[kind].at[me_d, zz, qq, low:high, :]

    def line_of(phase, kind, d, qq):
        low, high = spans[phase][kind]
        return (w_buf, o_buf)[kind].at[d, :, qq, low:high, :]

    def pass_on(phase, zz, qq, to_z, to_q):
        for kind in range(2):
            block = part(phase, kind, zz, qq)
            sem = w_recv.at[2 * phase + kind, zz, qq]
            copy(block, block, sem, (me_d, to_z * quad + to_q))

    def landed(phase, zz, qq):
        for kind in range(2):
            await_into(part(phase, kind, zz, qq), w_recv.at[2 * phase + kind, zz, qq])

    def to_mates(phase, qq):
        for kind in range(2):
            block = line_of(phase, kind, me_d, qq)
            for d in mates:
                copy(block, block, w_share.at[2 * phase + kind, me_d, qq], (d, me))

    def spread_own(phase):
        for k in range(1, line):
            pass_on(phase, z, q, lax.rem(z + k, line), q)
        pass_on(phase, z, q, z, x_side)
        pass_on(phase, z, q, z, y_side)

    def spread_line(phase):
        for k in range(1, line):
            zz = lax.rem(z + line - k, line)
            landed(phase, zz, q)
            pass_on(phase, zz, q, z, x_side)
            pass_on(phase, zz, q, z, y_side)
        to_mates(phase, q)

    def spread_far(phase):
        for k in range(line):
            zz = lax.rem(z + line - k, line)
            landed(phase, zz, x_side)
            landed(phase, zz, y_side)
            if k % 2 == 0:
                pass_on(phase, zz, x_side, z, y_side)
            else:
                pass_on(phase, zz, y_side, z, x_side)
        to_mates(phase, x_side)
        to_mates(phase, y_side)

    def finish(phase):
        for zz in range(line):
            landed(phase, zz, far)
        to_mates(phase, far)
        for d in mates:
            for qq in range(quad):
                for kind in range(2):
                    await_into(
                        line_of(phase, kind, d, qq), w_share.at[2 * phase + kind, d, qq]
                    )

    for buf, time_ref, space_ref in ((w_buf, wt_ref, ws_ref), (o_buf, ot_ref, os_ref)):
        count, depth = time_ref.shape[0], buf.shape[3]
        place_time = one_hot(count, depth, lambda r: r)
        place_space = one_hot(count, depth, lambda r: r + count)
        block = mm_tn(place_time, time_ref[...]) + mm_tn(place_space, space_ref[...])
        buf[me_d, z, q] = block.astype(BF16)

    def piece(o):
        return one_hot(
            tokens,
            n * slot,
            lambda t: (t % spots // per) * slot + (o * frames + t // spots) * per + t % per,
        )

    def arrival(o):
        return one_hot(tokens, n * slot, lambda r: (r // half) * slot + o * half + r % half)

    spots_first, spots_second = piece(0), piece(1)
    packed = mm_tn(spots_first, y1_ref[...]) + mm_tn(spots_second, g2_ref[...])
    sent[...] = packed.astype(BF16).reshape(sent.shape)

    pl.semaphore_wait(barrier, n - 1 + ndp - 1)

    def exchange(source, target, row):
        for s in others:
            copy(source.at[s], target.at[me], p_recv.at[row, me], (me_d, s))
        target[me] = source[me]

    def exchanged(target, row):
        for s in others:
            await_into(target.at[s], p_recv.at[row, s])

    spread_own(0)
    exchange(sent, arrived, 0)
    spread_line(0)
    spread_far(0)
    finish(0)
    spread_own(1)
    exchanged(arrived, 0)

    def groups(mark):
        row = mark(lax.broadcasted_iota(jnp.int32, (tokens, 1), 0))
        column = mark(lax.broadcasted_iota(jnp.int32, (1, tokens), 1))
        return row == column

    def weights(buf, low, high):
        def one(d):
            return lambda: buf[d, :, :, low:high, :].reshape(n * (high - low), buf.shape[4])

        return [one(d) for d in range(ndp)]

    def spreads(low_in, depth_in, low_out, depth_out):
        return (
            one_hot(width, n * depth_in, lambda c: c // rows_in * depth_in + low_in + c % rows_in),
            one_hot(WIDE, n * depth_out, lambda c: c // rows_out * depth_out + low_out + c % rows_out),
        )

    rows = arrived[...].reshape(n * slot, width)
    take_first, take_second = arrival(0), arrival(1)
    cotangent = mm(take_second, rows)
    w_in, w_out = weights(w_buf, 0, first_in), weights(o_buf, 0, first_out)
    spread_in, spread_out = spreads(0, first_in, 0, first_out)
    result, mixed, saved = forward(
        mm(take_first, rows), w_in, w_out, spread_in, spread_out, groups(lambda r: r % per)
    )
    spread_line(1)
    back = backward(saved, cotangent, w_in, w_out, spread_in, spread_out).astype(BF16)
    packed = mm_tn(take_first, result) + mm_tn(take_second, back)
    answer[...] = packed.astype(BF16).reshape(answer.shape)
    exchange(answer, returned, 1)
    for d, piece_of in enumerate(columns_of([cotangent], ndp)):
        g_part[d] = mm_tn(mixed, piece_of.astype(BF16)).astype(BF16)
    for d in mates:
        copy(g_part.at[d], g_chip.at[me_d], g_share.at[me_d], (d, me))
    g_chip[me_d] = g_part[me_d]
    spread_far(1)
    for d in mates:
        await_into(g_chip.at[d], g_share.at[d])
    total = g_chip[0].astype(F32)
    for d in range(1, ndp):
        total = total + g_chip[d].astype(F32)
    g_sent[...] = total.astype(BF16).reshape(g_sent.shape)
    exchange(g_sent, g_arrived, 2)

    exchanged(returned, 1)
    rows = returned[...].reshape(n * slot, width)
    x_second = (y2_ref[...].astype(F32) - mm(spots_first, rows)).astype(BF16)
    x2_ref[...] = x_second
    d_first = (g1_ref[...].astype(F32) + mm(spots_second, rows)).astype(BF16)
    d1_ref[...] = d_first
    finish(1)
    low_in, low_out = rows_in // 16 * 16, rows_out // 16 * 16
    high_in, high_out = whole(2 * rows_in), whole(2 * rows_out)
    w_in, w_out = weights(w_buf, low_in, high_in), weights(o_buf, low_out, high_out)
    spread_in, spread_out = spreads(
        rows_in - low_in, high_in - low_in, rows_out - low_out, high_out - low_out
    )
    result, _, saved = forward(
        x_second.astype(F32), w_in, w_out, spread_in, spread_out, groups(lambda t: t // spots)
    )
    x1_ref[...] = (y1_ref[...].astype(F32) - result.astype(F32)).astype(BF16)
    back = backward(saved, d_first.astype(F32), w_in, w_out, spread_in, spread_out)
    d2_ref[...] = (g2_ref[...].astype(F32) + back.astype(BF16).astype(F32)).astype(BF16)
    exchanged(g_arrived, 2)
    gw_ref[...] = jnp.sum(g_arrived[...].astype(F32), axis=0)[:rows_out]
    for made in pending:
        made.wait_send()


def body(n, ndp, *operands):
    shape = operands[0].shape
    frames, spots, width = shape[1:]
    tokens = frames * spots
    rows_in, columns_in = operands[4].shape
    rows_out, columns_out = operands[5].shape
    quad = 4 if n % 4 == 0 else 1
    line = n // quad
    slot = whole(2 * frames * spots // n)
    first_out = whole(rows_out)
    grad_rows = n * first_out
    per_phase = line - 1 + 2 + 2 * (line - 1) + line + quad * (ndp - 1)
    sends = 4 * per_phase + 3 * (n - 1) + ndp - 1
    like = jax.ShapeDtypeStruct((tokens, width), BF16)
    spec = pl.BlockSpec(memory_space=pltpu.VMEM)
    dma = pltpu.SemaphoreType.DMA
    outs = pl.pallas_call(
        functools.partial(block_kernel, n, ndp, frames, spots, rows_in, rows_out),
        out_shape=(like,) * 4 + (jax.ShapeDtypeStruct((rows_out, columns_out), F32),),
        in_specs=[spec] * 8,
        out_specs=[spec] * 5,
        scratch_shapes=[
            pltpu.VMEM((ndp, line, quad, whole(2 * rows_in), columns_in), BF16),
            pltpu.VMEM((ndp, line, quad, whole(2 * rows_out), columns_out), BF16),
            pltpu.VMEM((n, slot, width), BF16),
            pltpu.VMEM((n, slot, width), BF16),
            pltpu.VMEM((n, slot, width), BF16),
            pltpu.VMEM((n, slot, width), BF16),
            pltpu.VMEM((ndp, grad_rows, columns_out), BF16),
            pltpu.VMEM((ndp, grad_rows, columns_out), BF16),
            pltpu.VMEM((n, first_out, columns_out), BF16),
            pltpu.VMEM((n, first_out, columns_out), BF16),
            dma((4, line, quad)),
            dma((4, ndp, quad)),
            dma((3, n)),
            dma((ndp,)),
            dma((sends,)),
        ],
        compiler_params=pltpu.CompilerParams(
            collective_id=0, has_side_effects=True, vmem_limit_bytes=60 * 2**20
        ),
    )(*[part.reshape(tokens, width) for part in operands[:4]], *operands[4:])
    return tuple(part.reshape(shape) for part in outs[:4]) + (outs[4],)


def by_head(values, tokens):
    column = lax.broadcasted_iota(jnp.int32, (tokens, WIDE), 1)
    zero = jnp.zeros_like(values)
    return jnp.concatenate(
        [
            jnp.where((column >= h * HD) & (column < (h + 1) * HD), values, zero)
            for h in range(HEADS)
        ],
        axis=0,
    )


def side_by_side(stacked, tokens):
    return jnp.concatenate(
        [stacked[h * tokens : (h + 1) * tokens] for h in range(HEADS)], axis=1
    )


def solution(mesh):
    tokens = P("dp", "seq", None, None)
    weights = P("seq", "dp")
    return jax.shard_map(
        functools.partial(body, mesh.shape["seq"], mesh.shape["dp"]),
        mesh=mesh,
        in_specs=(tokens,) * 4 + (weights,) * 4,
        out_specs=(tokens,) * 4 + (weights,),
        check_vma=False,
    )
```

```python
import functools
import math

import jax
import jax.numpy as jnp
from jax import lax
from jax.experimental import pallas as pl
from jax.experimental.pallas import tpu as pltpu
from jax.sharding import PartitionSpec as P

HEADS = 8
HD = 72
WIDE = HEADS * HD
F32 = jnp.float32
BF16 = jnp.bfloat16
MESH = pl.DeviceIdType.MESH


def mm(a, b):
    return lax.dot_general(a, b, (((1,), (0,)), ((), ())), preferred_element_type=F32)


def mm_nt(a, b):
    return lax.dot_general(a, b, (((1,), (1,)), ((), ())), preferred_element_type=F32)


def mm_tn(a, b):
    return lax.dot_general(a, b, (((0,), (0,)), ((), ())), preferred_element_type=F32)


def whole(count):
    return (count + 15) // 16 * 16


def one_hot(rows, columns, target):
    place = target(lax.broadcasted_iota(jnp.int32, (rows, 1), 0))
    column = lax.broadcasted_iota(jnp.int32, (rows, columns), 1)
    return jnp.where(column == place, 1.0, 0.0).astype(BF16)


def columns_of(parts, count):
    joined = jnp.concatenate(parts, axis=1) if len(parts) > 1 else parts[0]
    each = joined.shape[1] // count
    return [joined[:, i * each : (i + 1) * each] for i in range(count)]


def forward(x, w_in, w_out, spread_in, spread_out, same, ready_in, between, ready_out):
    tokens = x.shape[0]
    scale = lax.rsqrt(jnp.mean(x * x, axis=-1, keepdims=True) + 1e-06)
    normed = mm((x * scale).astype(BF16), spread_in).astype(BF16)
    ready_in()
    query, keys, values = columns_of([mm(normed, w()) for w in w_in], 3)
    query = by_head(query, tokens).astype(BF16)
    scores = mm_nt(query, keys.astype(BF16)) * (1.0 / math.sqrt(HD))
    between()
    scores = scores.reshape(HEADS, tokens, tokens)
    scores = jnp.where(same[None], scores, -1e30)
    expo = jnp.exp(scores - jnp.max(scores, axis=-1, keepdims=True))
    exact = expo / jnp.sum(expo, axis=-1, keepdims=True)
    probs = exact.reshape(HEADS * tokens, tokens).astype(BF16)
    mixed = mm(side_by_side(probs, tokens), by_head(values, tokens).astype(BF16)).astype(BF16)
    spaced = mm(mixed, spread_out).astype(BF16)
    ready_out()
    result = columns_of([mm(spaced, w()) for w in w_out], 1)[0].astype(BF16)
    return result, mixed, (x, scale, query, keys, values.astype(BF16), probs)


def backward(saved, cotangent, w_in, w_out, spread_in, spread_out):
    x, scale, query, keys, values, probs = saved
    tokens = x.shape[0]
    pieces = columns_of([cotangent], len(w_out))
    d_mixed = sum(mm_nt(piece.astype(BF16), w()) for piece, w in zip(pieces, w_out))
    d_mixed = by_head(mm_nt(d_mixed.astype(BF16), spread_out), tokens).astype(BF16)
    d_values = mm_tn(probs, d_mixed)
    d_probs = mm_nt(d_mixed, values)
    weight = probs.astype(F32)
    inner = jnp.sum(d_probs * weight, axis=-1, keepdims=True)
    d_scores = (weight * (d_probs - inner) * (1.0 / math.sqrt(HD))).astype(BF16)
    d_query = mm(side_by_side(d_scores, tokens), by_head(keys, tokens).astype(BF16))
    d_keys = mm_tn(d_scores, query)
    pieces = columns_of([d_query, d_keys, d_values], len(w_in))
    d_normed = sum(mm_nt(piece.astype(BF16), w()) for piece, w in zip(pieces, w_in))
    d_normed = mm_nt(d_normed.astype(BF16), spread_in)
    inner = jnp.mean(d_normed * x, axis=-1, keepdims=True)
    return d_normed * scale - x * (scale * scale * scale * inner)


def block_kernel(
    n, ndp, frames, spots, rows_in, rows_out,
    y1_ref, y2_ref, g1_ref, g2_ref, ws_ref, os_ref, wt_ref, ot_ref, out_ref, gw_ref,
    w_buf, o_buf, sent, arrived, answer, returned, g_part, g_chip, g_sent, g_quad, g_mid, g_line,
    w_recv, w_share, p_recv, g_share, g_recv, send_sems,
):
    quad = 4 if n % 4 == 0 else 1
    line = n // quad
    me_d, me = lax.axis_index("dp"), lax.axis_index("seq")
    z, q = me // quad, me % quad
    x_side, y_side = q + 1 - 2 * (q % 2), (q + 2) % quad
    far = (x_side + 2) % quad
    tokens, width = y1_ref.shape
    per = spots // n
    half = frames * per
    slot = sent.shape[1]
    others = [lax.rem(me + k, n) for k in range(1, n)]
    mates = [lax.rem(me_d + k, ndp) for k in range(1, ndp)]
    first_in, first_out = whole(rows_in), whole(rows_out)
    phases = [
        (w_buf, 0, first_in),
        (o_buf, 0, first_out),
        (w_buf, first_in, w_buf.shape[3]),
        (o_buf, first_out, o_buf.shape[3]),
    ]
    pending = []

    barrier = pltpu.get_barrier_semaphore()
    for s in others:
        pl.semaphore_signal(barrier, inc=1, device_id=(me_d, s), device_id_type=MESH)
    for d in mates:
        pl.semaphore_signal(barrier, inc=1, device_id=(d, me), device_id_type=MESH)

    def copy(source, target, sem, device):
        made = pltpu.make_async_remote_copy(
            src_ref=source, dst_ref=target, send_sem=send_sems.at[len(pending)],
            recv_sem=sem, device_id=device, device_id_type=MESH,
        )
        made.start()
        pending.append(made)

    def await_into(target, sem):
        pltpu.make_async_remote_copy(
            src_ref=target, dst_ref=target, send_sem=send_sems.at[0], recv_sem=sem,
            device_id=(me_d, others[0]), device_id_type=MESH,
        ).wait_recv()

    def part(phase, zz, qq):
        buf, low, high = phases[phase]
        return buf.at[me_d, zz, qq, low:high, :]

    def line_of(phase, d, qq):
        buf, low, high = phases[phase]
        return buf.at[d, :, qq, low:high, :]

    def pass_on(phase, zz, qq, to_z, to_q):
        block = part(phase, zz, qq)
        copy(block, block, w_recv.at[phase, zz, qq], (me_d, to_z * quad + to_q))

    def landed(phase, zz, qq):
        await_into(part(phase, zz, qq), w_recv.at[phase, zz, qq])

    def to_mates(phase, qq):
        block = line_of(phase, me_d, qq)
        for d in mates:
            copy(block, block, w_share.at[phase, me_d, qq], (d, me))

    def own_line(phase):
        for k in range(1, line):
            pass_on(phase, z, q, lax.rem(z + k, line), q)

    def own_sides(phase):
        pass_on(phase, z, q, z, x_side)
        pass_on(phase, z, q, z, y_side)

    def spread_line(phase):
        for k in range(1, line):
            zz = lax.rem(z + line - k, line)
            landed(phase, zz, q)
            pass_on(phase, zz, q, z, x_side)
            pass_on(phase, zz, q, z, y_side)
        to_mates(phase, q)

    def spread_far(phase):
        for k in range(line):
            zz = lax.rem(z + line - k, line)
            landed(phase, zz, x_side)
            landed(phase, zz, y_side)
            if k % 2 == 0:
                pass_on(phase, zz, x_side, z, y_side)
            else:
                pass_on(phase, zz, y_side, z, x_side)
        to_mates(phase, x_side)
        to_mates(phase, y_side)

    def finish(phase):
        for zz in range(line):
            landed(phase, zz, far)
        to_mates(phase, far)
        for d in mates:
            for qq in range(quad):
                await_into(line_of(phase, d, qq), w_share.at[phase, d, qq])

    for buf, time_ref, space_ref in ((w_buf, wt_ref, ws_ref), (o_buf, ot_ref, os_ref)):
        count, depth = time_ref.shape[0], buf.shape[3]
        place_time = one_hot(count, depth, lambda r: r)
        place_space = one_hot(count, depth, lambda r: r + count)
        block = mm_tn(place_time, time_ref[...]) + mm_tn(place_space, space_ref[...])
        buf[me_d, z, q] = block.astype(BF16)

    def piece(o):
        return one_hot(
            tokens,
            n * slot,
            lambda t: (t % spots // per) * slot + (o * frames + t // spots) * per + t % per,
        )

    def arrival(o):
        return one_hot(tokens, n * slot, lambda r: (r // half) * slot + o * half + r % half)

    def exchange(source, target, row):
        for s in others:
            copy(source.at[s], target.at[me], p_recv.at[row, me], (me_d, s))
        target[me] = source[me]

    def exchanged(target, row):
        for s in others:
            await_into(target.at[s], p_recv.at[row, s])

    def groups(mark):
        row = mark(lax.broadcasted_iota(jnp.int32, (tokens, 1), 0))
        column = mark(lax.broadcasted_iota(jnp.int32, (1, tokens), 1))
        return row == column

    def weights(buf, low, high):
        def one(d):
            return lambda: buf[d, :, :, low:high, :].reshape(n * (high - low), buf.shape[4])

        return [one(d) for d in range(ndp)]

    def spreads(low_in, depth_in, low_out, depth_out):
        return (
            one_hot(width, n * depth_in, lambda c: c // rows_in * depth_in + low_in + c % rows_in),
            one_hot(WIDE, n * depth_out, lambda c: c // rows_out * depth_out + low_out + c % rows_out),
        )

    pl.semaphore_wait(barrier, n - 1 + ndp - 1)
    own_line(0)
    own_sides(0)
    spots_first, spots_second = piece(0), piece(1)
    packed = mm_tn(spots_first, y1_ref[...]) + mm_tn(spots_second, g2_ref[...])
    sent[...] = packed.astype(BF16).reshape(sent.shape)
    exchange(sent, arrived, 0)
    own_line(1)
    spread_in, spread_out = spreads(0, first_in, 0, first_out)
    spread_line(0)
    own_line(2)
    own_line(3)
    spread_far(0)
    own_sides(1)
    spread_line(1)

    exchanged(arrived, 0)
    rows = arrived[...].reshape(n * slot, width)
    take_first, take_second = arrival(0), arrival(1)
    cotangent = mm(take_second, rows)

    def next_phases():
        spread_far(1)
        own_sides(2)
        spread_line(2)
        own_sides(3)
        spread_line(3)

    w_in, w_out = weights(w_buf, 0, first_in), weights(o_buf, 0, first_out)
    result, mixed, saved = forward(
        mm(take_first, rows), w_in, w_out, spread_in, spread_out, groups(lambda r: r % per),
        lambda: finish(0), next_phases, lambda: finish(1),
    )
    back = backward(saved, cotangent, w_in, w_out, spread_in, spread_out).astype(BF16)
    packed = mm_tn(take_first, result) + mm_tn(take_second, back)
    answer[...] = packed.astype(BF16).reshape(answer.shape)
    exchange(answer, returned, 1)

    depth = g_sent.shape[1]
    by_quad = one_hot(
        WIDE,
        quad * depth,
        lambda c: c // rows_out % quad * depth + c // (rows_out * quad) * rows_out + c % rows_out,
    )
    mixed = mm(mixed, by_quad).astype(BF16)
    for d, piece_of in enumerate(columns_of([cotangent], ndp)):
        g_part[d] = mm_tn(mixed, piece_of.astype(BF16)).astype(BF16).reshape(g_part.shape[1:])
    for d in mates:
        copy(g_part.at[d], g_chip.at[me_d], g_share.at[me_d], (d, me))
    g_chip[me_d] = g_part[me_d]
    spread_far(2)
    for d in mates:
        await_into(g_chip.at[d], g_share.at[d])
    total = g_chip[0].astype(F32)
    for d in range(1, ndp):
        total = total + g_chip[d].astype(F32)
    g_sent[...] = total.astype(BF16)
    for k in range(1, quad):
        qq = lax.rem(q + k, quad)
        copy(g_sent.at[qq], g_quad.at[q], g_recv.at[q], (me_d, z * quad + qq))
    g_quad[q] = g_sent[q]
    low_in, low_out = rows_in // 16 * 16, rows_out // 16 * 16
    high_in, high_out = whole(2 * rows_in), whole(2 * rows_out)
    spread_in, spread_out = spreads(
        rows_in - low_in, high_in - low_in, rows_out - low_out, high_out - low_out
    )
    spread_far(3)

    exchanged(returned, 1)
    rows = returned[...].reshape(n * slot, width)
    x_second = (y2_ref[...].astype(F32) - mm(spots_first, rows)).astype(BF16)
    out_ref[1] = x_second
    d_first = (g1_ref[...].astype(F32) + mm(spots_second, rows)).astype(BF16)
    out_ref[2] = d_first

    def sum_quad():
        for k in range(1, quad):
            qq = lax.rem(q + k, quad)
            await_into(g_quad.at[qq], g_recv.at[qq])
        total = jnp.sum(g_quad[...].astype(F32), axis=0).astype(BF16)
        regroup = one_hot(
            depth, line * first_out, lambda r: r // rows_out * first_out + r % rows_out
        )
        g_mid[...] = mm_tn(regroup, total).astype(BF16).reshape(g_mid.shape)
        for k in range(1, line):
            zz = lax.rem(z + k, line)
            copy(g_mid.at[zz], g_line.at[z], g_recv.at[quad + z], (me_d, zz * quad + q))
        g_line[z] = g_mid[z]

    w_in, w_out = weights(w_buf, low_in, high_in), weights(o_buf, low_out, high_out)
    result, _, saved = forward(
        x_second.astype(F32), w_in, w_out, spread_in, spread_out, groups(lambda t: t // spots),
        lambda: finish(2), sum_quad, lambda: finish(3),
    )
    out_ref[0] = (y1_ref[...].astype(F32) - result.astype(F32)).astype(BF16)
    back = backward(saved, d_first.astype(F32), w_in, w_out, spread_in, spread_out)
    out_ref[3] = (g2_ref[...].astype(F32) + back.astype(BF16).astype(F32)).astype(BF16)
    for k in range(1, line):
        zz = lax.rem(z + k, line)
        await_into(g_line.at[zz], g_recv.at[quad + zz])
    gw_ref[...] = jnp.sum(g_line[...].astype(F32), axis=0)[:rows_out]
    for made in pending:
        made.wait_send()


def body(n, ndp, *operands):
    shape = operands[0].shape
    frames, spots, width = shape[1:]
    tokens = frames * spots
    rows_in, columns_in = operands[4].shape
    rows_out, columns_out = operands[5].shape
    quad = 4 if n % 4 == 0 else 1
    line = n // quad
    slot = whole(2 * frames * spots // n)
    first_out = whole(rows_out)
    depth = whole(line * rows_out)
    per_phase = line - 1 + 2 + 2 * (line - 1) + line + quad * (ndp - 1)
    sends = 4 * per_phase + 2 * (n - 1) + ndp - 1 + quad - 1 + line - 1
    spec = pl.BlockSpec(memory_space=pltpu.VMEM)
    dma = pltpu.SemaphoreType.DMA
    stacked, grad = pl.pallas_call(
        functools.partial(block_kernel, n, ndp, frames, spots, rows_in, rows_out),
        out_shape=(
            jax.ShapeDtypeStruct((4, tokens, width), BF16),
            jax.ShapeDtypeStruct((rows_out, columns_out), F32),
        ),
        in_specs=[spec] * 8,
        out_specs=[spec] * 2,
        scratch_shapes=[
            pltpu.VMEM((ndp, line, quad, whole(2 * rows_in), columns_in), BF16),
            pltpu.VMEM((ndp, line, quad, whole(2 * rows_out), columns_out), BF16),
            pltpu.VMEM((n, slot, width), BF16),
            pltpu.VMEM((n, slot, width), BF16),
            pltpu.VMEM((n, slot, width), BF16),
            pltpu.VMEM((n, slot, width), BF16),
            pltpu.VMEM((ndp, quad, depth, columns_out), BF16),
            pltpu.VMEM((ndp, quad, depth, columns_out), BF16),
            pltpu.VMEM((quad, depth, columns_out), BF16),
            pltpu.VMEM((quad, depth, columns_out), BF16),
            pltpu.VMEM((line, first_out, columns_out), BF16),
            pltpu.VMEM((line, first_out, columns_out), BF16),
            dma((4, line, quad)),
            dma((4, ndp, quad)),
            dma((2, n)),
            dma((ndp,)),
            dma((quad + line,)),
            dma((sends,)),
        ],
        compiler_params=pltpu.CompilerParams(
            collective_id=0, has_side_effects=True, vmem_limit_bytes=60 * 2**20
        ),
    )(*[part.reshape(tokens, width) for part in operands[:4]], *operands[4:])
    return tuple(stacked[i].reshape(shape) for i in range(4)) + (grad,)


def by_head(values, tokens):
    column = lax.broadcasted_iota(jnp.int32, (tokens, WIDE), 1)
    zero = jnp.zeros_like(values)
    return jnp.concatenate(
        [
            jnp.where((column >= h * HD) & (column < (h + 1) * HD), values, zero)
            for h in range(HEADS)
        ],
        axis=0,
    )


def side_by_side(stacked, tokens):
    return jnp.concatenate(
        [stacked[h * tokens : (h + 1) * tokens] for h in range(HEADS)], axis=1
    )


def solution(mesh):
    tokens = P("dp", "seq", None, None)
    weights = P("seq", "dp")
    return jax.shard_map(
        functools.partial(body, mesh.shape["seq"], mesh.shape["dp"]),
        mesh=mesh,
        in_specs=(tokens,) * 4 + (weights,) * 4,
        out_specs=(tokens,) * 4 + (weights,),
        check_vma=False,
    )
```

```python
import functools
import math

import jax
import jax.numpy as jnp
from jax import lax
from jax.experimental import pallas as pl
from jax.experimental.pallas import tpu as pltpu
from jax.sharding import PartitionSpec as P

HEADS = 8
HD = 72
WIDE = HEADS * HD
F32 = jnp.float32
BF16 = jnp.bfloat16
MESH = pl.DeviceIdType.MESH


def mm(a, b):
    return lax.dot_general(a, b, (((1,), (0,)), ((), ())), preferred_element_type=F32)


def mm_nt(a, b):
    return lax.dot_general(a, b, (((1,), (1,)), ((), ())), preferred_element_type=F32)


def mm_tn(a, b):
    return lax.dot_general(a, b, (((0,), (0,)), ((), ())), preferred_element_type=F32)


def whole(count):
    return (count + 15) // 16 * 16


def one_hot(rows, columns, target):
    place = target(lax.broadcasted_iota(jnp.int32, (rows, 1), 0))
    column = lax.broadcasted_iota(jnp.int32, (rows, columns), 1)
    return jnp.where(column == place, 1.0, 0.0).astype(BF16)


def columns_of(parts, count):
    joined = jnp.concatenate(parts, axis=1) if len(parts) > 1 else parts[0]
    each = joined.shape[1] // count
    return [joined[:, i * each : (i + 1) * each] for i in range(count)]


def forward(x, w_in, w_out, spread_in, spread_out, same, ready_in, between, ready_out):
    tokens = x.shape[0]
    scale = lax.rsqrt(jnp.mean(x * x, axis=-1, keepdims=True) + 1e-06)
    normed = mm((x * scale).astype(BF16), spread_in).astype(BF16)
    ready_in()
    query, keys, values = columns_of([mm(normed, w()) for w in w_in], 3)
    query = by_head(query, tokens).astype(BF16)
    scores = mm_nt(query, keys.astype(BF16)) * (1.0 / math.sqrt(HD))
    between()
    scores = scores.reshape(HEADS, tokens, tokens)
    scores = jnp.where(same[None], scores, -1e30)
    expo = jnp.exp(scores - jnp.max(scores, axis=-1, keepdims=True))
    exact = expo / jnp.sum(expo, axis=-1, keepdims=True)
    probs = exact.reshape(HEADS * tokens, tokens).astype(BF16)
    mixed = mm(side_by_side(probs, tokens), by_head(values, tokens).astype(BF16)).astype(BF16)
    spaced = mm(mixed, spread_out).astype(BF16)
    ready_out()
    result = columns_of([mm(spaced, w()) for w in w_out], 1)[0].astype(BF16)
    return result, mixed, (x, scale, query, keys, values.astype(BF16), probs)


def backward(saved, cotangent, w_in, w_out, spread_in, spread_out):
    x, scale, query, keys, values, probs = saved
    tokens = x.shape[0]
    pieces = columns_of([cotangent], len(w_out))
    d_mixed = sum(mm_nt(piece.astype(BF16), w()) for piece, w in zip(pieces, w_out))
    d_mixed = by_head(mm_nt(d_mixed.astype(BF16), spread_out), tokens).astype(BF16)
    d_values = mm_tn(probs, d_mixed)
    d_probs = mm_nt(d_mixed, values)
    weight = probs.astype(F32)
    inner = jnp.sum(d_probs * weight, axis=-1, keepdims=True)
    d_scores = (weight * (d_probs - inner) * (1.0 / math.sqrt(HD))).astype(BF16)
    d_query = mm(side_by_side(d_scores, tokens), by_head(keys, tokens).astype(BF16))
    d_keys = mm_tn(d_scores, query)
    pieces = columns_of([d_query, d_keys, d_values], len(w_in))
    d_normed = sum(mm_nt(piece.astype(BF16), w()) for piece, w in zip(pieces, w_in))
    d_normed = mm_nt(d_normed.astype(BF16), spread_in)
    inner = jnp.mean(d_normed * x, axis=-1, keepdims=True)
    return d_normed * scale - x * (scale * scale * scale * inner)


def block_kernel(
    n, ndp, frames, spots, rows_in, rows_out,
    y1_ref, y2_ref, g1_ref, g2_ref, ws_ref, os_ref, wt_ref, ot_ref, out_ref, gw_ref,
    w_buf, o_buf, sent, arrived, answer, returned, g_part, g_chip, g_sent, g_quad, g_mid, g_line,
    w_recv, w_share, p_recv, g_share, g_recv, send_sems,
):
    quad = 4 if n % 4 == 0 else 1
    line = n // quad
    me_d, me = lax.axis_index("dp"), lax.axis_index("seq")
    z, q = me // quad, me % quad
    x_side, y_side = q + 1 - 2 * (q % 2), (q + 2) % quad
    far = (x_side + 2) % quad
    tokens, width = y1_ref.shape
    per = spots // n
    half = frames * per
    slot = sent.shape[1]
    others = [lax.rem(me + k, n) for k in range(1, n)]
    mates = [lax.rem(me_d + k, ndp) for k in range(1, ndp)]
    first_in, first_out = whole(rows_in), whole(rows_out)
    phases = [
        (w_buf, 0, first_in),
        (o_buf, 0, first_out),
        (w_buf, first_in, w_buf.shape[3]),
        (o_buf, first_out, o_buf.shape[3]),
    ]
    pending = []

    barrier = pltpu.get_barrier_semaphore()
    for s in others:
        pl.semaphore_signal(barrier, inc=1, device_id=(me_d, s), device_id_type=MESH)
    for d in mates:
        pl.semaphore_signal(barrier, inc=1, device_id=(d, me), device_id_type=MESH)

    def copy(source, target, sem, device):
        made = pltpu.make_async_remote_copy(
            src_ref=source, dst_ref=target, send_sem=send_sems.at[len(pending)],
            recv_sem=sem, device_id=device, device_id_type=MESH,
        )
        made.start()
        pending.append(made)

    def await_into(target, sem):
        pltpu.make_async_remote_copy(
            src_ref=target, dst_ref=target, send_sem=send_sems.at[0], recv_sem=sem,
            device_id=(me_d, others[0]), device_id_type=MESH,
        ).wait_recv()

    def part(phase, zz, qq):
        buf, low, high = phases[phase]
        return buf.at[me_d, zz, qq, low:high, :]

    def line_of(phase, d, qq):
        buf, low, high = phases[phase]
        return buf.at[d, :, qq, low:high, :]

    def pass_on(phase, zz, qq, to_z, to_q):
        block = part(phase, zz, qq)
        copy(block, block, w_recv.at[phase, zz, qq], (me_d, to_z * quad + to_q))

    def landed(phase, zz, qq):
        await_into(part(phase, zz, qq), w_recv.at[phase, zz, qq])

    def to_mates(phase, qq):
        block = line_of(phase, me_d, qq)
        for d in mates:
            copy(block, block, w_share.at[phase, me_d, qq], (d, me))

    def own_line(phase):
        for k in range(1, line):
            pass_on(phase, z, q, lax.rem(z + k, line), q)

    def own_sides(phase):
        pass_on(phase, z, q, z, x_side)
        pass_on(phase, z, q, z, y_side)

    def spread_line(phase):
        for k in range(1, line):
            zz = lax.rem(z + line - k, line)
            landed(phase, zz, q)
            pass_on(phase, zz, q, z, x_side)
            pass_on(phase, zz, q, z, y_side)
        to_mates(phase, q)

    def spread_far(phase):
        for k in range(line):
            zz = lax.rem(z + line - k, line)
            landed(phase, zz, x_side)
            landed(phase, zz, y_side)
            if k % 2 == 0:
                pass_on(phase, zz, x_side, z, y_side)
            else:
                pass_on(phase, zz, y_side, z, x_side)
        to_mates(phase, x_side)
        to_mates(phase, y_side)

    def finish(phase):
        for zz in range(line):
            landed(phase, zz, far)
        to_mates(phase, far)
        for d in mates:
            for qq in range(quad):
                await_into(line_of(phase, d, qq), w_share.at[phase, d, qq])

    for buf, time_ref, space_ref in ((w_buf, wt_ref, ws_ref), (o_buf, ot_ref, os_ref)):
        count, depth = time_ref.shape[0], buf.shape[3]
        place_time = one_hot(count, depth, lambda r: r)
        place_space = one_hot(count, depth, lambda r: r + count)
        block = mm_tn(place_time, time_ref[...]) + mm_tn(place_space, space_ref[...])
        buf[me_d, z, q] = block.astype(BF16)

    def piece(o):
        return one_hot(
            tokens,
            n * slot,
            lambda t: (t % spots // per) * slot + (o * frames + t // spots) * per + t % per,
        )

    def arrival(o):
        return one_hot(tokens, n * slot, lambda r: (r // half) * slot + o * half + r % half)

    def exchange(source, target, row):
        for s in others:
            copy(source.at[s], target.at[me], p_recv.at[row, me], (me_d, s))
        target[me] = source[me]

    def exchanged(target, row):
        for s in others:
            await_into(target.at[s], p_recv.at[row, s])

    def groups(mark):
        row = mark(lax.broadcasted_iota(jnp.int32, (tokens, 1), 0))
        column = mark(lax.broadcasted_iota(jnp.int32, (1, tokens), 1))
        return row == column

    def weights(buf, low, high):
        def one(d):
            return lambda: buf[d, :, :, low:high, :].reshape(n * (high - low), buf.shape[4])

        return [one(d) for d in range(ndp)]

    def spreads(low_in, depth_in, low_out, depth_out):
        return (
            one_hot(width, n * depth_in, lambda c: c // rows_in * depth_in + low_in + c % rows_in),
            one_hot(WIDE, n * depth_out, lambda c: c // rows_out * depth_out + low_out + c % rows_out),
        )

    pl.semaphore_wait(barrier, n - 1 + ndp - 1)
    own_line(0)
    own_sides(0)
    spots_first, spots_second = piece(0), piece(1)
    packed = mm_tn(spots_first, y1_ref[...]) + mm_tn(spots_second, g2_ref[...])
    sent[...] = packed.astype(BF16).reshape(sent.shape)
    spread_in, spread_out = spreads(0, first_in, 0, first_out)
    spread_line(0)
    exchange(sent, arrived, 0)
    own_line(1)
    own_line(2)
    own_line(3)
    spread_far(0)
    own_sides(1)
    spread_line(1)

    exchanged(arrived, 0)
    rows = arrived[...].reshape(n * slot, width)
    take_first, take_second = arrival(0), arrival(1)
    cotangent = mm(take_second, rows)

    def next_phases():
        spread_far(1)
        own_sides(2)
        spread_line(2)
        own_sides(3)
        spread_line(3)

    w_in, w_out = weights(w_buf, 0, first_in), weights(o_buf, 0, first_out)
    result, mixed, saved = forward(
        mm(take_first, rows), w_in, w_out, spread_in, spread_out, groups(lambda r: r % per),
        lambda: finish(0), next_phases, lambda: finish(1),
    )
    back = backward(saved, cotangent, w_in, w_out, spread_in, spread_out).astype(BF16)
    packed = mm_tn(take_first, result) + mm_tn(take_second, back)
    answer[...] = packed.astype(BF16).reshape(answer.shape)
    exchange(answer, returned, 1)

    depth = g_sent.shape[1]
    by_quad = one_hot(
        WIDE,
        quad * depth,
        lambda c: c // rows_out % quad * depth + c // (rows_out * quad) * rows_out + c % rows_out,
    )
    mixed = mm(mixed, by_quad).astype(BF16)
    for d, piece_of in enumerate(columns_of([cotangent], ndp)):
        g_part[d] = mm_tn(mixed, piece_of.astype(BF16)).astype(BF16).reshape(g_part.shape[1:])
    for d in mates:
        copy(g_part.at[d], g_chip.at[me_d], g_share.at[me_d], (d, me))
    g_chip[me_d] = g_part[me_d]
    spread_far(2)
    for d in mates:
        await_into(g_chip.at[d], g_share.at[d])
    total = g_chip[0].astype(F32)
    for d in range(1, ndp):
        total = total + g_chip[d].astype(F32)
    g_sent[...] = total.astype(BF16)
    low_in, low_out = rows_in // 16 * 16, rows_out // 16 * 16
    high_in, high_out = whole(2 * rows_in), whole(2 * rows_out)
    spread_in, spread_out = spreads(
        rows_in - low_in, high_in - low_in, rows_out - low_out, high_out - low_out
    )
    spread_far(3)

    exchanged(returned, 1)
    rows = returned[...].reshape(n * slot, width)
    x_second = (y2_ref[...].astype(F32) - mm(spots_first, rows)).astype(BF16)
    out_ref[1] = x_second
    d_first = (g1_ref[...].astype(F32) + mm(spots_second, rows)).astype(BF16)
    out_ref[2] = d_first

    def send_quad():
        finish(2)
        for k in range(1, quad):
            qq = lax.rem(q + k, quad)
            copy(g_sent.at[qq], g_quad.at[q], g_recv.at[q], (me_d, z * quad + qq))
        g_quad[q] = g_sent[q]

    def sum_quad():
        for k in range(1, quad):
            qq = lax.rem(q + k, quad)
            await_into(g_quad.at[qq], g_recv.at[qq])
        total = jnp.sum(g_quad[...].astype(F32), axis=0).astype(BF16)
        regroup = one_hot(
            depth, line * first_out, lambda r: r // rows_out * first_out + r % rows_out
        )
        g_mid[...] = mm_tn(regroup, total).astype(BF16).reshape(g_mid.shape)
        for k in range(1, line):
            zz = lax.rem(z + k, line)
            copy(g_mid.at[zz], g_line.at[z], g_recv.at[quad + z], (me_d, zz * quad + q))
        g_line[z] = g_mid[z]

    w_in, w_out = weights(w_buf, low_in, high_in), weights(o_buf, low_out, high_out)
    result, _, saved = forward(
        x_second.astype(F32), w_in, w_out, spread_in, spread_out, groups(lambda t: t // spots),
        send_quad, lambda: None, lambda: finish(3),
    )
    sum_quad()
    out_ref[0] = (y1_ref[...].astype(F32) - result.astype(F32)).astype(BF16)
    back = backward(saved, d_first.astype(F32), w_in, w_out, spread_in, spread_out)
    out_ref[3] = (g2_ref[...].astype(F32) + back.astype(BF16).astype(F32)).astype(BF16)
    for k in range(1, line):
        zz = lax.rem(z + k, line)
        await_into(g_line.at[zz], g_recv.at[quad + zz])
    gw_ref[...] = jnp.sum(g_line[...].astype(F32), axis=0)[:rows_out]
    for made in pending:
        made.wait_send()


def body(n, ndp, *operands):
    shape = operands[0].shape
    frames, spots, width = shape[1:]
    tokens = frames * spots
    rows_in, columns_in = operands[4].shape
    rows_out, columns_out = operands[5].shape
    quad = 4 if n % 4 == 0 else 1
    line = n // quad
    slot = whole(2 * frames * spots // n)
    first_out = whole(rows_out)
    depth = whole(line * rows_out)
    per_phase = line - 1 + 2 + 2 * (line - 1) + line + quad * (ndp - 1)
    sends = 4 * per_phase + 2 * (n - 1) + ndp - 1 + quad - 1 + line - 1
    spec = pl.BlockSpec(memory_space=pltpu.VMEM)
    dma = pltpu.SemaphoreType.DMA
    stacked, grad = pl.pallas_call(
        functools.partial(block_kernel, n, ndp, frames, spots, rows_in, rows_out),
        out_shape=(
            jax.ShapeDtypeStruct((4, tokens, width), BF16),
            jax.ShapeDtypeStruct((rows_out, columns_out), F32),
        ),
        in_specs=[spec] * 8,
        out_specs=[spec] * 2,
        scratch_shapes=[
            pltpu.VMEM((ndp, line, quad, whole(2 * rows_in), columns_in), BF16),
            pltpu.VMEM((ndp, line, quad, whole(2 * rows_out), columns_out), BF16),
            pltpu.VMEM((n, slot, width), BF16),
            pltpu.VMEM((n, slot, width), BF16),
            pltpu.VMEM((n, slot, width), BF16),
            pltpu.VMEM((n, slot, width), BF16),
            pltpu.VMEM((ndp, quad, depth, columns_out), BF16),
            pltpu.VMEM((ndp, quad, depth, columns_out), BF16),
            pltpu.VMEM((quad, depth, columns_out), BF16),
            pltpu.VMEM((quad, depth, columns_out), BF16),
            pltpu.VMEM((line, first_out, columns_out), BF16),
            pltpu.VMEM((line, first_out, columns_out), BF16),
            dma((4, line, quad)),
            dma((4, ndp, quad)),
            dma((2, n)),
            dma((ndp,)),
            dma((quad + line,)),
            dma((sends,)),
        ],
        compiler_params=pltpu.CompilerParams(
            collective_id=0, has_side_effects=True, vmem_limit_bytes=60 * 2**20
        ),
    )(*[part.reshape(tokens, width) for part in operands[:4]], *operands[4:])
    return tuple(stacked[i].reshape(shape) for i in range(4)) + (grad,)


def by_head(values, tokens):
    column = lax.broadcasted_iota(jnp.int32, (tokens, WIDE), 1)
    zero = jnp.zeros_like(values)
    return jnp.concatenate(
        [
            jnp.where((column >= h * HD) & (column < (h + 1) * HD), values, zero)
            for h in range(HEADS)
        ],
        axis=0,
    )


def side_by_side(stacked, tokens):
    return jnp.concatenate(
        [stacked[h * tokens : (h + 1) * tokens] for h in range(HEADS)], axis=1
    )


def solution(mesh):
    tokens = P("dp", "seq", None, None)
    weights = P("seq", "dp")
    return jax.shard_map(
        functools.partial(body, mesh.shape["seq"], mesh.shape["dp"]),
        mesh=mesh,
        in_specs=(tokens,) * 4 + (weights,) * 4,
        out_specs=(tokens,) * 4 + (weights,),
        check_vma=False,
    )
```

```python
import functools
import math

import jax
import jax.numpy as jnp
from jax import lax
from jax.experimental import pallas as pl
from jax.experimental.pallas import tpu as pltpu
from jax.sharding import PartitionSpec as P

HEADS = 8
HD = 72
WIDE = HEADS * HD
F32 = jnp.float32
BF16 = jnp.bfloat16
MESH = pl.DeviceIdType.MESH


def mm(a, b):
    return lax.dot_general(a, b, (((1,), (0,)), ((), ())), preferred_element_type=F32)


def mm_nt(a, b):
    return lax.dot_general(a, b, (((1,), (1,)), ((), ())), preferred_element_type=F32)


def mm_tn(a, b):
    return lax.dot_general(a, b, (((0,), (0,)), ((), ())), preferred_element_type=F32)


def whole(count):
    return (count + 15) // 16 * 16


def one_hot(rows, columns, target):
    place = target(lax.broadcasted_iota(jnp.int32, (rows, 1), 0))
    column = lax.broadcasted_iota(jnp.int32, (rows, columns), 1)
    return jnp.where(column == place, 1.0, 0.0).astype(BF16)


def columns_of(parts, count):
    joined = jnp.concatenate(parts, axis=1) if len(parts) > 1 else parts[0]
    each = joined.shape[1] // count
    return [joined[:, i * each : (i + 1) * each] for i in range(count)]


def forward(x, w_in, w_out, spread_in, spread_out, same, ready_in, between, ready_out):
    tokens = x.shape[0]
    scale = lax.rsqrt(jnp.mean(x * x, axis=-1, keepdims=True) + 1e-06)
    normed = mm((x * scale).astype(BF16), spread_in).astype(BF16)
    ready_in()
    query, keys, values = columns_of([mm(normed, w()) for w in w_in], 3)
    query = by_head(query, tokens).astype(BF16)
    scores = mm_nt(query, keys.astype(BF16)) * (1.0 / math.sqrt(HD))
    between()
    scores = scores.reshape(HEADS, tokens, tokens)
    scores = jnp.where(same[None], scores, -1e30)
    expo = jnp.exp(scores - jnp.max(scores, axis=-1, keepdims=True))
    exact = expo / jnp.sum(expo, axis=-1, keepdims=True)
    probs = exact.reshape(HEADS * tokens, tokens).astype(BF16)
    mixed = mm(side_by_side(probs, tokens), by_head(values, tokens).astype(BF16)).astype(BF16)
    spaced = mm(mixed, spread_out).astype(BF16)
    ready_out()
    result = columns_of([mm(spaced, w()) for w in w_out], 1)[0].astype(BF16)
    return result, mixed, (x, scale, query, keys, values.astype(BF16), probs)


def backward(saved, cotangent, w_in, w_out, spread_in, spread_out):
    x, scale, query, keys, values, probs = saved
    tokens = x.shape[0]
    pieces = columns_of([cotangent], len(w_out))
    d_mixed = sum(mm_nt(piece.astype(BF16), w()) for piece, w in zip(pieces, w_out))
    d_mixed = by_head(mm_nt(d_mixed.astype(BF16), spread_out), tokens).astype(BF16)
    d_values = mm_tn(probs, d_mixed)
    d_probs = mm_nt(d_mixed, values)
    weight = probs.astype(F32)
    inner = jnp.sum(d_probs * weight, axis=-1, keepdims=True)
    d_scores = (weight * (d_probs - inner) * (1.0 / math.sqrt(HD))).astype(BF16)
    d_query = mm(side_by_side(d_scores, tokens), by_head(keys, tokens).astype(BF16))
    d_keys = mm_tn(d_scores, query)
    pieces = columns_of([d_query, d_keys, d_values], len(w_in))
    d_normed = sum(mm_nt(piece.astype(BF16), w()) for piece, w in zip(pieces, w_in))
    d_normed = mm_nt(d_normed.astype(BF16), spread_in)
    inner = jnp.mean(d_normed * x, axis=-1, keepdims=True)
    return d_normed * scale - x * (scale * scale * scale * inner)


def block_kernel(
    n, ndp, frames, spots, rows_in, rows_out,
    y1_ref, y2_ref, g1_ref, g2_ref, ws_ref, os_ref, wt_ref, ot_ref, out_ref, gw_ref,
    w_buf, o_buf, sent, arrived, answer, returned, g_part, g_chip, g_sent, g_quad, g_mid, g_line,
    w_recv, w_share, p_recv, g_share, g_recv, send_sems,
):
    quad = 4 if n % 4 == 0 else 1
    line = n // quad
    me_d, me = lax.axis_index("dp"), lax.axis_index("seq")
    z, q = me // quad, me % quad
    x_side, y_side = q + 1 - 2 * (q % 2), (q + 2) % quad
    far = (x_side + 2) % quad
    tokens, width = y1_ref.shape
    per = spots // n
    half = frames * per
    slot = sent.shape[1]
    others = [lax.rem(me + k, n) for k in range(1, n)]
    mates = [lax.rem(me_d + k, ndp) for k in range(1, ndp)]
    first_in, first_out = whole(rows_in), whole(rows_out)
    phases = [
        (w_buf, 0, first_in),
        (o_buf, 0, first_out),
        (w_buf, first_in, w_buf.shape[3]),
        (o_buf, first_out, o_buf.shape[3]),
    ]
    pending = []

    barrier = pltpu.get_barrier_semaphore()
    for s in others:
        pl.semaphore_signal(barrier, inc=1, device_id=(me_d, s), device_id_type=MESH)
    for d in mates:
        pl.semaphore_signal(barrier, inc=1, device_id=(d, me), device_id_type=MESH)

    def copy(source, target, sem, device):
        made = pltpu.make_async_remote_copy(
            src_ref=source, dst_ref=target, send_sem=send_sems.at[len(pending)],
            recv_sem=sem, device_id=device, device_id_type=MESH,
        )
        made.start()
        pending.append(made)

    def await_into(target, sem):
        pltpu.make_async_remote_copy(
            src_ref=target, dst_ref=target, send_sem=send_sems.at[0], recv_sem=sem,
            device_id=(me_d, others[0]), device_id_type=MESH,
        ).wait_recv()

    def part(phase, zz, qq):
        buf, low, high = phases[phase]
        return buf.at[me_d, zz, qq, low:high, :]

    def line_of(phase, d, qq):
        buf, low, high = phases[phase]
        return buf.at[d, :, qq, low:high, :]

    def pass_on(phase, zz, qq, to_z, to_q):
        block = part(phase, zz, qq)
        copy(block, block, w_recv.at[phase, zz, qq], (me_d, to_z * quad + to_q))

    def landed(phase, zz, qq):
        await_into(part(phase, zz, qq), w_recv.at[phase, zz, qq])

    def to_mates(phase, qq):
        block = line_of(phase, me_d, qq)
        for d in mates:
            copy(block, block, w_share.at[phase, me_d, qq], (d, me))

    def own_line(phase):
        for k in range(1, line):
            pass_on(phase, z, q, lax.rem(z + k, line), q)

    def own_sides(phase):
        pass_on(phase, z, q, z, x_side)
        pass_on(phase, z, q, z, y_side)

    def spread_line(phase):
        for k in range(1, line):
            zz = lax.rem(z + line - k, line)
            landed(phase, zz, q)
            pass_on(phase, zz, q, z, x_side)
            pass_on(phase, zz, q, z, y_side)
        to_mates(phase, q)

    def spread_far(phase):
        for k in range(line):
            zz = lax.rem(z + line - k, line)
            landed(phase, zz, x_side)
            landed(phase, zz, y_side)
            if k % 2 == 0:
                pass_on(phase, zz, x_side, z, y_side)
            else:
                pass_on(phase, zz, y_side, z, x_side)
        to_mates(phase, x_side)
        to_mates(phase, y_side)

    def finish(phase):
        for zz in range(line):
            landed(phase, zz, far)
        to_mates(phase, far)
        for d in mates:
            for qq in range(quad):
                await_into(line_of(phase, d, qq), w_share.at[phase, d, qq])

    for buf, time_ref, space_ref in ((w_buf, wt_ref, ws_ref), (o_buf, ot_ref, os_ref)):
        count, depth = time_ref.shape[0], buf.shape[3]
        place_time = one_hot(count, depth, lambda r: r)
        place_space = one_hot(count, depth, lambda r: r + count)
        block = mm_tn(place_time, time_ref[...]) + mm_tn(place_space, space_ref[...])
        buf[me_d, z, q] = block.astype(BF16)

    def piece(o):
        return one_hot(
            tokens,
            n * slot,
            lambda t: (t % spots // per) * slot + (o * frames + t // spots) * per + t % per,
        )

    def arrival(o):
        return one_hot(tokens, n * slot, lambda r: (r // half) * slot + o * half + r % half)

    def exchange(source, target, row):
        for s in others:
            copy(source.at[s], target.at[me], p_recv.at[row, me], (me_d, s))
        target[me] = source[me]

    def exchanged(target, row):
        for s in others:
            await_into(target.at[s], p_recv.at[row, s])

    def groups(mark):
        row = mark(lax.broadcasted_iota(jnp.int32, (tokens, 1), 0))
        column = mark(lax.broadcasted_iota(jnp.int32, (1, tokens), 1))
        return row == column

    def weights(buf, low, high):
        def one(d):
            return lambda: buf[d, :, :, low:high, :].reshape(n * (high - low), buf.shape[4])

        return [one(d) for d in range(ndp)]

    def spreads(low_in, depth_in, low_out, depth_out):
        return (
            one_hot(width, n * depth_in, lambda c: c // rows_in * depth_in + low_in + c % rows_in),
            one_hot(WIDE, n * depth_out, lambda c: c // rows_out * depth_out + low_out + c % rows_out),
        )

    pl.semaphore_wait(barrier, n - 1 + ndp - 1)
    own_line(0)
    own_sides(0)
    spots_first, spots_second = piece(0), piece(1)
    packed = mm_tn(spots_first, y1_ref[...]) + mm_tn(spots_second, g2_ref[...])
    sent[...] = packed.astype(BF16).reshape(sent.shape)
    exchange(sent, arrived, 0)
    own_line(1)
    spread_in, spread_out = spreads(0, first_in, 0, first_out)
    spread_line(0)
    own_line(2)
    own_line(3)
    spread_far(0)
    own_sides(1)
    spread_line(1)

    exchanged(arrived, 0)
    rows = arrived[...].reshape(n * slot, width)
    take_first, take_second = arrival(0), arrival(1)
    cotangent = mm(take_second, rows)

    def next_phases():
        spread_far(1)
        own_sides(2)
        own_sides(3)

    w_in, w_out = weights(w_buf, 0, first_in), weights(o_buf, 0, first_out)
    result, mixed, saved = forward(
        mm(take_first, rows), w_in, w_out, spread_in, spread_out, groups(lambda r: r % per),
        lambda: finish(0), next_phases, lambda: finish(1),
    )
    spread_line(2)
    back = backward(saved, cotangent, w_in, w_out, spread_in, spread_out).astype(BF16)
    packed = mm_tn(take_first, result) + mm_tn(take_second, back)
    answer[...] = packed.astype(BF16).reshape(answer.shape)
    exchange(answer, returned, 1)
    spread_line(3)

    depth = g_sent.shape[1]
    by_quad = one_hot(
        WIDE,
        quad * depth,
        lambda c: c // rows_out % quad * depth + c // (rows_out * quad) * rows_out + c % rows_out,
    )
    mixed = mm(mixed, by_quad).astype(BF16)
    for d, piece_of in enumerate(columns_of([cotangent], ndp)):
        g_part[d] = mm_tn(mixed, piece_of.astype(BF16)).astype(BF16).reshape(g_part.shape[1:])
    for d in mates:
        copy(g_part.at[d], g_chip.at[me_d], g_share.at[me_d], (d, me))
    g_chip[me_d] = g_part[me_d]
    spread_far(2)
    for d in mates:
        await_into(g_chip.at[d], g_share.at[d])
    total = g_chip[0].astype(F32)
    for d in range(1, ndp):
        total = total + g_chip[d].astype(F32)
    g_sent[...] = total.astype(BF16)
    for k in range(1, quad):
        qq = lax.rem(q + k, quad)
        copy(g_sent.at[qq], g_quad.at[q], g_recv.at[q], (me_d, z * quad + qq))
    g_quad[q] = g_sent[q]
    low_in, low_out = rows_in // 16 * 16, rows_out // 16 * 16
    high_in, high_out = whole(2 * rows_in), whole(2 * rows_out)
    spread_in, spread_out = spreads(
        rows_in - low_in, high_in - low_in, rows_out - low_out, high_out - low_out
    )
    spread_far(3)

    exchanged(returned, 1)
    rows = returned[...].reshape(n * slot, width)
    x_second = (y2_ref[...].astype(F32) - mm(spots_first, rows)).astype(BF16)
    out_ref[1] = x_second
    d_first = (g1_ref[...].astype(F32) + mm(spots_second, rows)).astype(BF16)
    out_ref[2] = d_first

    def sum_quad():
        for k in range(1, quad):
            qq = lax.rem(q + k, quad)
            await_into(g_quad.at[qq], g_recv.at[qq])
        total = jnp.sum(g_quad[...].astype(F32), axis=0).astype(BF16)
        regroup = one_hot(
            depth, line * first_out, lambda r: r // rows_out * first_out + r % rows_out
        )
        g_mid[...] = mm_tn(regroup, total).astype(BF16).reshape(g_mid.shape)
        for k in range(1, line):
            zz = lax.rem(z + k, line)
            copy(g_mid.at[zz], g_line.at[z], g_recv.at[quad + z], (me_d, zz * quad + q))
        g_line[z] = g_mid[z]

    w_in, w_out = weights(w_buf, low_in, high_in), weights(o_buf, low_out, high_out)
    result, _, saved = forward(
        x_second.astype(F32), w_in, w_out, spread_in, spread_out, groups(lambda t: t // spots),
        lambda: finish(2), sum_quad, lambda: finish(3),
    )
    out_ref[0] = (y1_ref[...].astype(F32) - result.astype(F32)).astype(BF16)
    back = backward(saved, d_first.astype(F32), w_in, w_out, spread_in, spread_out)
    out_ref[3] = (g2_ref[...].astype(F32) + back.astype(BF16).astype(F32)).astype(BF16)
    for k in range(1, line):
        zz = lax.rem(z + k, line)
        await_into(g_line.at[zz], g_recv.at[quad + zz])
    gw_ref[...] = jnp.sum(g_line[...].astype(F32), axis=0)[:rows_out]
    for made in pending:
        made.wait_send()


def body(n, ndp, *operands):
    shape = operands[0].shape
    frames, spots, width = shape[1:]
    tokens = frames * spots
    rows_in, columns_in = operands[4].shape
    rows_out, columns_out = operands[5].shape
    quad = 4 if n % 4 == 0 else 1
    line = n // quad
    slot = whole(2 * frames * spots // n)
    first_out = whole(rows_out)
    depth = whole(line * rows_out)
    per_phase = line - 1 + 2 + 2 * (line - 1) + line + quad * (ndp - 1)
    sends = 4 * per_phase + 2 * (n - 1) + ndp - 1 + quad - 1 + line - 1
    spec = pl.BlockSpec(memory_space=pltpu.VMEM)
    dma = pltpu.SemaphoreType.DMA
    stacked, grad = pl.pallas_call(
        functools.partial(block_kernel, n, ndp, frames, spots, rows_in, rows_out),
        out_shape=(
            jax.ShapeDtypeStruct((4, tokens, width), BF16),
            jax.ShapeDtypeStruct((rows_out, columns_out), F32),
        ),
        in_specs=[spec] * 8,
        out_specs=[spec] * 2,
        scratch_shapes=[
            pltpu.VMEM((ndp, line, quad, whole(2 * rows_in), columns_in), BF16),
            pltpu.VMEM((ndp, line, quad, whole(2 * rows_out), columns_out), BF16),
            pltpu.VMEM((n, slot, width), BF16),
            pltpu.VMEM((n, slot, width), BF16),
            pltpu.VMEM((n, slot, width), BF16),
            pltpu.VMEM((n, slot, width), BF16),
            pltpu.VMEM((ndp, quad, depth, columns_out), BF16),
            pltpu.VMEM((ndp, quad, depth, columns_out), BF16),
            pltpu.VMEM((quad, depth, columns_out), BF16),
            pltpu.VMEM((quad, depth, columns_out), BF16),
            pltpu.VMEM((line, first_out, columns_out), BF16),
            pltpu.VMEM((line, first_out, columns_out), BF16),
            dma((4, line, quad)),
            dma((4, ndp, quad)),
            dma((2, n)),
            dma((ndp,)),
            dma((quad + line,)),
            dma((sends,)),
        ],
        compiler_params=pltpu.CompilerParams(
            collective_id=0, has_side_effects=True, vmem_limit_bytes=60 * 2**20
        ),
    )(*[part.reshape(tokens, width) for part in operands[:4]], *operands[4:])
    return tuple(stacked[i].reshape(shape) for i in range(4)) + (grad,)


def by_head(values, tokens):
    column = lax.broadcasted_iota(jnp.int32, (tokens, WIDE), 1)
    zero = jnp.zeros_like(values)
    return jnp.concatenate(
        [
            jnp.where((column >= h * HD) & (column < (h + 1) * HD), values, zero)
            for h in range(HEADS)
        ],
        axis=0,
    )


def side_by_side(stacked, tokens):
    return jnp.concatenate(
        [stacked[h * tokens : (h + 1) * tokens] for h in range(HEADS)], axis=1
    )


def solution(mesh):
    tokens = P("dp", "seq", None, None)
    weights = P("seq", "dp")
    return jax.shard_map(
        functools.partial(body, mesh.shape["seq"], mesh.shape["dp"]),
        mesh=mesh,
        in_specs=(tokens,) * 4 + (weights,) * 4,
        out_specs=(tokens,) * 4 + (weights,),
        check_vma=False,
    )
```
